32 devices in a mesh: grp: 2 (over y), row: 4 (over x, core), col: 4 (over z).
Axes of the slice: x: 2, y: 2, z: 4, core: 2. Of those that a mesh axis runs over, the one named last changes fastest.
Arguments:
- level_one: bfloat16 [128, 256, 192], P(('grp', 'row'), 'col'), parts along dimension 0, may hold values from -6 to 6
- level_two: bfloat16 [64, 128, 384], P(('grp', 'row'), 'col'), parts along dimension 0, may hold values from -6 to 6
- level_three: bfloat16 [32, 64, 768], P(('grp', 'row'), None, 'col'), parts along dimension 0, may hold values from -6 to 6
- level_four: bfloat16 [16, 32, 1536], P(('grp', 'row'), None, 'col'), parts along dimension 0, may hold values from -10.5 to 10.5
- bin_weight: bfloat16 [4, 1536, 256], P(None, 'col'), may hold values from -0.21875 to 0.21875
- neck_feature: bfloat16 [3, 3, 1536, 256], P(None, None, 'col'), may hold values from -0.0546875 to 0.0546875
- neck_pooled: bfloat16 [3, 3, 1024, 256], P(None, None, 'col'), may hold values from -0.0546875 to 0.0546875
- lateral_one: bfloat16 [192, 256], replicated, may hold values from -0.625 to 0.625
- lateral_two: bfloat16 [384, 256], replicated, may hold values from -0.4375 to 0.4375
- lateral_three: bfloat16 [768, 256], replicated, may hold values from -0.3125 to 0.3125
- smooth_weight: bfloat16 [3, 3, 3, 256, 256], replicated, may hold values from -0.1875 to 0.1875
- join_weight: bfloat16 [3, 3, 1024, 256], replicated, may hold values from -0.09375 to 0.09375
- biases: float32 [12, 256], replicated, may hold values from -2 to 2
Outputs:
- joined: bfloat16 [128, 256, 256], P(('grp', 'row'), 'col'), parts along dimension 0
The draws below stay inside these ranges and needn't reach their ends.
There are 2 independent parts, one for each index of `grp`. The reference program is written for one: setup_inputs(seed, part) draws one part's arguments, and reference() takes and returns one part's arrays. A program takes and returns all parts, laid end to end along the dimension named above; an argument that names none is the same for every part. Nothing has to cross between parts.
All inputs are finite; a program needn't handle non-finite values.
Results may differ from the reference program's by a relative error of at most 0.015.
Values may be sent and summed in bfloat16 or wider, within the bound.
A program may use at most 64 MiB of HBM per device.

```python
import math
import jax
import jax.numpy as jnp
from jax import lax

C1 = 192
C2 = 384
C3 = 768
C4 = 1536
CH = 256
NH1 = 64
NW1 = 256
NH2 = 32
NW2 = 128
NH3 = 16
NW3 = 64
NH4 = 8
NW4 = 32


def draw_level_four(key, part):
    pieces = jax.random.split(jax.random.fold_in(key, 41), 6)
    shape = (NH4, NW4, C4)
    down = jnp.arange(NH4, dtype=jnp.float32)[:, None, None]
    across = jnp.arange(NW4, dtype=jnp.float32)[None, :, None]
    level_mean = jnp.clip(jax.random.normal(pieces[1], (C4,), jnp.float32), -3.0, 3.0)
    wave_size = jnp.clip(jax.random.normal(pieces[2], (C4,), jnp.float32), -2.0, 2.0)
    freq_down = jax.random.randint(pieces[3], (C4,), 1, 4).astype(jnp.float32)
    freq_across = jax.random.randint(pieces[4], (C4,), 0, 4).astype(jnp.float32)
    phase = jax.random.uniform(pieces[5], (C4,), jnp.float32, -math.pi, math.pi)
    noise = 0.6 * jnp.clip(jax.random.normal(pieces[0], shape, jnp.float32), -4.0, 4.0)
    trend = 0.5 + 1.5 * down / NH4
    wave = jnp.cos(2.0 * math.pi * (freq_down * down / NH4 + freq_across * across / NW4) + phase)
    return (noise + level_mean * trend + wave_size * wave).astype(jnp.bfloat16)


def level_of(key, shape, cuts, smallest, high):
    def one(dim, shards_of):
        heights = jax.random.uniform(jax.random.fold_in(jax.random.fold_in(key, 6), dim), (shards_of,), jnp.float32, smallest / len(cuts), high / len(cuts))
        return jnp.repeat(jnp.exp(heights), shape[dim] // shards_of).reshape((-1,) + (1,) * (len(shape) - dim - 1))

    loudness = one(*cuts[0])
    for cut in cuts[1:]:
        loudness = loudness * one(*cut)
    return loudness


def normal_values(key, dims, deviation, limit, cuts=(), kind=jnp.bfloat16):
    factor_of = level_of(key, dims, cuts, -0.22, 0.18) if cuts else 1.0
    array = jax.random.normal(key, dims, jnp.float32) * deviation * factor_of
    return jnp.minimum(jnp.maximum(array, -limit), limit).astype(kind)


def setup_inputs(seed: int = 0, part: int = 0) -> dict:
    seeds = jax.random.split(jax.random.key(seed), 14)
    part_keys = jax.random.split(jax.random.fold_in(seeds[13], part), 14)
    level_one = normal_values(part_keys[0], (NH1, NW1, C1), 1.0, 6.0, ((0, 4), (1, 4)))
    level_two = normal_values(part_keys[1], (NH2, NW2, C2), 1.0, 6.0, ((0, 4), (1, 4)))
    level_three = normal_values(part_keys[2], (NH3, NW3, C3), 1.0, 6.0, ((0, 4), (2, 4)))
    level_four = draw_level_four(jax.random.fold_in(jax.random.fold_in(seeds[13], part), 71), part)
    bin_weight = normal_values(seeds[4], (4, C4, CH), (C4 // 2) ** -0.5, 0.21875, ((1, 4),))
    neck_feature = normal_values(seeds[5], (3, 3, C4, CH), (9 * (C4 + 4 * CH) // 2) ** -0.5, 0.0546875, ((2, 4),))
    neck_pooled = normal_values(seeds[6], (3, 3, 4 * CH, CH), (9 * (C4 + 4 * CH) // 2) ** -0.5, 0.0546875, ((2, 4),))
    lateral_one = normal_values(seeds[7], (C1, CH), (C1 // 2) ** -0.5, 0.625)
    lateral_two = normal_values(seeds[8], (C2, CH), (C2 // 2) ** -0.5, 0.4375)
    lateral_three = normal_values(seeds[9], (C3, CH), (C3 // 2) ** -0.5, 0.3125)
    smooth_weight = normal_values(seeds[10], (3, 3, 3, CH, CH), (9 * CH // 2) ** -0.5, 0.1875)
    join_weight = normal_values(seeds[11], (3, 3, 4 * CH, CH), (9 * 4 * CH // 2) ** -0.5, 0.09375)
    biases = normal_values(seeds[12], (12, CH), 0.3, 2.0, (), jnp.float32)
    return dict(level_one=level_one, level_two=level_two, level_three=level_three, level_four=level_four, bin_weight=bin_weight, neck_feature=neck_feature, neck_pooled=neck_pooled, lateral_one=lateral_one, lateral_two=lateral_two, lateral_three=lateral_three, smooth_weight=smooth_weight, join_weight=join_weight, biases=biases)


highest = lax.Precision.HIGHEST
bin_sides = (1, 2, 3, 6)


def pool_matrix(bin_side, extent, first, length):
    cell_index = jnp.arange(bin_side, dtype=jnp.int32)[:, None]
    position = first + jnp.arange(length, dtype=jnp.int32)[None, :]
    cell_first = (cell_index * extent) // bin_side
    cell_end = ((cell_index + 1) * extent + bin_side - 1) // bin_side
    inside = (position >= cell_first) & (position < cell_end)
    return inside.astype(jnp.float32) / (cell_end - cell_first).astype(jnp.float32)


def stretch_rows(position, bin_side, extent):
    source = jnp.clip((position + 0.5) * bin_side / extent - 0.5, 0.0, bin_side - 1.0)
    targets = jnp.arange(bin_side, dtype=jnp.float32)[None, :]
    return jnp.maximum(0.0, 1.0 - jnp.abs(source[:, None] - targets))


def taps_sum(padded, weight):
    height = padded.shape[0] - 2
    breadth = padded.shape[1] - 2
    channels = padded.shape[2]
    summed = jnp.zeros((height * breadth, weight.shape[-1]), jnp.float32)
    for row_tap in range(3):
        for col_tap in range(3):
            window = padded[row_tap:row_tap + height, col_tap:col_tap + breadth].reshape(height * breadth, channels)
            summed = summed + jnp.dot(window, weight[row_tap, col_tap], preferred_element_type=jnp.float32)
    return summed.reshape(height, breadth, -1)


def conv_same(feature, weight):
    return taps_sum(jnp.pad(feature, ((1, 1), (1, 1), (0, 0))), weight)


def project(feature, weight):
    height, breadth, channels = feature.shape
    result = jnp.dot(feature.reshape(height * breadth, channels), weight, preferred_element_type=jnp.float32)
    return result.reshape(height, breadth, -1)


def upscale(feature, factor):
    height, breadth = feature.shape[0], feature.shape[1]
    row_weights = stretch_rows(jnp.arange(height * factor, dtype=jnp.float32), height, height * factor)
    col_weights = stretch_rows(jnp.arange(breadth * factor, dtype=jnp.float32), breadth, breadth * factor)
    result = jnp.einsum("oh,hwc->owc", row_weights, feature.astype(jnp.float32), precision=highest)
    return jnp.einsum("pw,owc->opc", col_weights, result, precision=highest)


def reference(level_one, level_two, level_three, level_four, bin_weight, neck_feature, neck_pooled,
              lateral_one, lateral_two, lateral_three, smooth_weight, join_weight, biases):
    grid_rows, grid_cols = level_four.shape[0], level_four.shape[1]
    coarse = level_four.astype(jnp.float32)
    bin_maps = []
    for number, bin_side in enumerate(bin_sides):
        pool_down = pool_matrix(bin_side, grid_rows, 0, grid_rows)
        pool_across = pool_matrix(bin_side, grid_cols, 0, grid_cols)
        pooled = jnp.einsum("ih,hwc->iwc", pool_down, coarse, precision=highest)
        pooled = jnp.einsum("jw,iwc->ijc", pool_across, pooled, precision=highest)
        mapped = jnp.einsum("ijc,cd->ijd", pooled, bin_weight[number].astype(jnp.float32), precision=highest)
        binned = jax.nn.relu(mapped + biases[number])
        stretch_down = stretch_rows(jnp.arange(grid_rows, dtype=jnp.float32), bin_side, grid_rows)
        stretch_across = stretch_rows(jnp.arange(grid_cols, dtype=jnp.float32), bin_side, grid_cols)
        spread = jnp.einsum("hi,ijd->hjd", stretch_down, binned, precision=highest)
        spread = jnp.einsum("wj,hjd->hwd", stretch_across, spread, precision=highest)
        bin_maps.append(spread)
    ppm_maps = jnp.concatenate(bin_maps, axis=2).astype(jnp.bfloat16)
    stacked = jnp.concatenate([level_four, ppm_maps], axis=2)
    neck_weight = jnp.concatenate([neck_feature, neck_pooled], axis=2)
    pyramid_four = jax.nn.relu(conv_same(stacked, neck_weight) + biases[4]).astype(jnp.bfloat16)
    pyramid_three = (jax.nn.relu(project(level_three, lateral_three) + biases[7])
                     + upscale(pyramid_four, 2)).astype(jnp.bfloat16)
    pyramid_two = (jax.nn.relu(project(level_two, lateral_two) + biases[6])
                   + upscale(pyramid_three, 2)).astype(jnp.bfloat16)
    pyramid_one = (jax.nn.relu(project(level_one, lateral_one) + biases[5])
                   + upscale(pyramid_two, 2)).astype(jnp.bfloat16)
    smooth_one = jax.nn.relu(conv_same(pyramid_one, smooth_weight[0]) + biases[8]).astype(jnp.bfloat16)
    smooth_two = jax.nn.relu(conv_same(pyramid_two, smooth_weight[1]) + biases[9]).astype(jnp.bfloat16)
    smooth_three = jax.nn.relu(conv_same(pyramid_three, smooth_weight[2]) + biases[10]).astype(jnp.bfloat16)
    stacked_top = jnp.concatenate([
        smooth_one,
        upscale(smooth_two, 2).astype(jnp.bfloat16),
        upscale(smooth_three, 4).astype(jnp.bfloat16),
        upscale(pyramid_four, 8).astype(jnp.bfloat16)], axis=2)
    return jax.nn.relu(conv_same(stacked_top, join_weight) + biases[11]).astype(jnp.bfloat16)
```

```python
import functools
import jax
import jax.numpy as jnp
import numpy as np
from jax import lax
from jax.experimental import pallas as pl
from jax.experimental.pallas import tpu as pltpu
from jax.sharding import PartitionSpec as P

bin_sides = (1, 2, 3, 6)
MESH = pl.DeviceIdType.MESH
EDGE = 16
CELLS = 48


def round_up(value, unit):
    return -(-value // unit) * unit


def pool_counts(rows, cols):
    member = np.zeros((len(bin_sides) * CELLS, rows * cols), np.float32)
    scale = np.zeros((len(bin_sides) * CELLS, 1), np.float32)
    for k, b in enumerate(bin_sides):
        for i in range(b):
            for j in range(b):
                r0, r1 = i * rows // b, -(-(i + 1) * rows // b)
                c0, c1 = j * cols // b, -(-(j + 1) * cols // b)
                cell = np.zeros((rows, cols), np.float32)
                cell[r0:r1, c0:c1] = 1.0
                member[k * CELLS + i * b + j] = cell.reshape(-1)
                scale[k * CELLS + i * b + j] = 1.0 / ((r1 - r0) * (c1 - c0))
    return member, scale


def stretch(count, bin_side):
    place = np.arange(count, dtype=np.float32)
    source = np.clip((place + 0.5) * bin_side / count - 0.5, 0.0, bin_side - 1.0)
    return np.maximum(0.0, 1.0 - np.abs(source[:, None] - np.arange(bin_side)[None, :]))


def spread_table(rows, cols, border):
    table = np.zeros((len(bin_sides), rows + 2 * border, cols, CELLS), np.float32)
    for k, b in enumerate(bin_sides):
        both = stretch(rows, b)[:, None, :, None] * stretch(cols, b)[None, :, None, :]
        table[k, border : border + rows, :, : b * b] = both.reshape(rows, cols, b * b)
    return table.reshape(len(bin_sides), (rows + 2 * border) * cols, CELLS)


def pick_table(rows, cols, parts, first, width):
    own = cols // parts
    table = np.zeros((parts, rows, width, rows, cols), np.float32)
    for part in range(parts):
        for j in range(width):
            source = part * own + first + j
            if 0 <= source < cols:
                for r in range(rows):
                    table[part, r, j, r, source] = 1.0
    return table.reshape(parts * rows * width, rows * cols)


def dot(a, b):
    return jnp.dot(a, b, preferred_element_type=jnp.float32)


def front(
    sizes, one, two, three, four, bins, neck, necked, offsets, bin_bias, member, scale, spread,
    pick_top, pick_three,
    f1, f2, t3, top,
    grid, rows3, send3, bin_out, bin_in, sendt, gott, ppm,
    sem_four, sem_row, sem_col, sem_three, sem_bin, sem_top,
):
    count_r, count_c = sizes
    row, col = lax.axis_index("row"), lax.axis_index("col")
    h1, w1, _ = one.shape
    h2, w2, _ = two.shape
    h3, w3, _ = three.shape
    h4, w4, c4 = four.shape
    share = necked.shape[2]
    channels = neck.shape[3]
    wide3 = t3.shape[1]
    wide_t = top.shape[0]
    border = 3

    for frame, block, h, w in ((f1, one, h1, w1), (f2, two, h2, w2)):
        depth = frame.shape[2]
        frame[0:2] = jnp.zeros((2, w + 2 * EDGE, depth), frame.dtype)
        frame[2 + h :] = jnp.zeros((2, w + 2 * EDGE, depth), frame.dtype)
        frame[2 : 2 + h, 0:EDGE] = jnp.zeros((h, EDGE, depth), frame.dtype)
        frame[2 : 2 + h, EDGE + w :] = jnp.zeros((h, EDGE, depth), frame.dtype)
    rows3[0:2] = jnp.zeros((2, w3, three.shape[2]), rows3.dtype)
    rows3[2 + h3 :] = jnp.zeros((2, w3, three.shape[2]), rows3.dtype)
    grid[0:border] = jnp.zeros((border, w4, c4), grid.dtype)
    grid[border + h4 * count_r :] = jnp.zeros((border, w4, c4), grid.dtype)

    barrier = pltpu.get_barrier_semaphore()
    for step in range(1, count_r):
        pl.semaphore_signal(
            barrier, inc=1, device_id={"row": lax.rem(row + step, count_r)}, device_id_type=MESH
        )
    for step in range(1, count_c):
        pl.semaphore_signal(
            barrier, inc=1, device_id={"col": lax.rem(col + step, count_c)}, device_id_type=MESH
        )
    pl.semaphore_wait(barrier, count_r + count_c - 2)

    def remote(source, target, sems, number, where):
        return pltpu.make_async_remote_copy(
            src_ref=source, dst_ref=target, send_sem=sems.at[0, number],
            recv_sem=sems.at[1, number], device_id=where, device_id_type=MESH,
        )

    four_copies = []
    for step in range(1, count_r):
        copy = remote(
            four, grid.at[pl.ds(border + row * h4, h4)], sem_four, step - 1,
            {"row": lax.rem(row + step, count_r)},
        )
        copy.start()
        four_copies.append(copy)
    up_copies, down_copies = [], []
    for number, (block, frame, h, w, left) in enumerate(
        ((three, rows3, h3, w3, 0), (one, f1, h1, w1, EDGE), (two, f2, h2, w2, EDGE))
    ):
        up_copies.append(
            remote(block.at[0:2], frame.at[2 + h : 4 + h, left : left + w], sem_row, number,
                   {"row": row - 1})
        )
        down_copies.append(
            remote(block.at[h - 2 : h], frame.at[0:2, left : left + w], sem_row, 3 + number,
                   {"row": row + 1})
        )

    @pl.when(row > 0)
    def _():
        for copy in up_copies:
            copy.start()

    @pl.when(row < count_r - 1)
    def _():
        for copy in down_copies:
            copy.start()

    grid[pl.ds(border + row * h4, h4)] = four[...]
    f1[2 : 2 + h1, EDGE : EDGE + w1] = one[...]
    f2[2 : 2 + h2, EDGE : EDGE + w2] = two[...]
    rows3[2 : 2 + h3] = three[...]
    for copy in four_copies:
        copy.wait_recv()

    whole = grid[border : border + h4 * count_r].reshape(h4 * count_r * w4, c4)
    pooled = dot(member[...], whole) * scale[...]
    high = pooled.astype(jnp.bfloat16)
    low = (pooled - high.astype(jnp.float32)).astype(jnp.bfloat16)
    for k in range(len(bin_sides)):
        rows = slice(k * CELLS, (k + 1) * CELLS)
        part = (dot(high[rows], bins[k]) + dot(low[rows], bins[k])).astype(jnp.bfloat16)
        for piece in range(channels // share):
            bin_out[k * (channels // share) + piece] = part[:, piece * share : (piece + 1) * share]
    bin_copies = []
    for step in range(1, count_c):
        there = lax.rem(col + step, count_c)
        copy = remote(bin_out.at[there], bin_in.at[col], sem_bin, step - 1, {"col": there})
        copy.start()
        bin_copies.append(copy)
    bin_in[pl.ds(col, 1)] = bin_out[pl.ds(col, 1)]

    @pl.when(row < count_r - 1)
    def _():
        for copy in up_copies:
            copy.wait_recv()

    @pl.when(row > 0)
    def _():
        for copy in down_copies:
            copy.wait_recv()

    left_copies, right_copies = [], []
    for number, (frame, w) in enumerate(((f1, w1), (f2, w2))):
        left_copies.append(
            remote(frame.at[:, EDGE : 2 * EDGE], frame.at[:, EDGE + w :], sem_col, number,
                   {"col": col - 1})
        )
        right_copies.append(
            remote(frame.at[:, w : EDGE + w], frame.at[:, 0:EDGE], sem_col, 2 + number,
                   {"col": col + 1})
        )

    @pl.when(col > 0)
    def _():
        for copy in left_copies:
            copy.start()

    @pl.when(col < count_c - 1)
    def _():
        for copy in right_copies:
            copy.start()

    tall3 = rows3[...].reshape((h3 + 4) * w3, three.shape[2])
    for part in range(count_c):
        send3[part] = dot(
            pick_three[part * wide3 : (part + 1) * wide3], tall3
        ).astype(jnp.bfloat16)
    three_copies = []
    for step in range(1, count_c):
        there = lax.rem(col + step, count_c)
        copy = remote(send3.at[there], t3.at[col], sem_three, step - 1, {"col": there})
        copy.start()
        three_copies.append(copy)
    t3[pl.ds(col, 1)] = send3[pl.ds(col, 1)]

    tall = h4 + 4
    terms = [None] * 3
    for dy in range(3):
        window = grid[pl.ds(row * h4 + dy, tall)].reshape(tall * w4, c4)
        for dx in range(3):
            term = dot(window, neck[dy, dx])
            terms[dx] = term if dy == 0 else terms[dx] + term

    for copy in bin_copies:
        copy.wait_recv()
    total = bin_in[0].astype(jnp.float32)
    for part in range(1, count_c):
        total = total + bin_in[part].astype(jnp.float32)
    binned = jnp.maximum(total + bin_bias[pl.ds(col, 1)].reshape(1, share), 0.0)
    branch = col * share // channels
    table = spread[branch, pl.ds(pl.multiple_of(row * h4 * w4, 8), (tall + 2) * w4), :]
    ppm[...] = (
        jnp.dot(table, binned, precision=lax.Precision.HIGHEST, preferred_element_type=jnp.float32)
        .astype(jnp.bfloat16)
        .reshape(tall + 2, w4, share)
    )
    for dy in range(3):
        window = ppm[dy : dy + tall].reshape(tall * w4, share)
        for dx in range(3):
            terms[dx] = terms[dx] + dot(window, necked[dy, dx])
    place = lax.rem(lax.broadcasted_iota(jnp.int32, (tall * w4, 1), 0), w4)
    partial = (
        terms[1]
        + jnp.where(place > 0, pltpu.roll(terms[0], 1, 0), 0.0)
        + jnp.where(place < w4 - 1, pltpu.roll(terms[2], tall * w4 - 1, 0), 0.0)
    ).astype(jnp.bfloat16)
    for part in range(count_c):
        sendt[part] = dot(pick_top[part * wide_t : (part + 1) * wide_t], partial).astype(
            jnp.bfloat16
        )
    top_copies = []
    for step in range(1, count_c):
        there = lax.rem(col + step, count_c)
        copy = remote(sendt.at[there], gott.at[col], sem_top, step - 1, {"col": there})
        copy.start()
        top_copies.append(copy)
    gott[pl.ds(col, 1)] = sendt[pl.ds(col, 1)]
    for copy in top_copies:
        copy.wait_recv()
    total = gott[0].astype(jnp.float32)
    for part in range(1, count_c):
        total = total + gott[part].astype(jnp.float32)
    top[...] = jnp.maximum(total + offsets[4:5], 0.0).astype(jnp.bfloat16)

    for copy in three_copies:
        copy.wait_recv()

    @pl.when(col < count_c - 1)
    def _():
        for copy in left_copies:
            copy.wait_recv()

    @pl.when(col > 0)
    def _():
        for copy in right_copies:
            copy.wait_recv()

    for copy in four_copies + bin_copies + three_copies + top_copies:
        copy.wait_send()

    @pl.when(row > 0)
    def _():
        for copy in up_copies:
            copy.wait_send()

    @pl.when(row < count_r - 1)
    def _():
        for copy in down_copies:
            copy.wait_send()

    @pl.when(col > 0)
    def _():
        for copy in left_copies:
            copy.wait_send()

    @pl.when(col < count_c - 1)
    def _():
        for copy in right_copies:
            copy.wait_send()


def column_matrix(col, own, first, width, own_from, first_from, width_from, factor, total):
    place = col * own + first + lax.broadcasted_iota(jnp.int32, (width, width_from), 0)
    source = (place.astype(jnp.float32) + 0.5) / factor - 0.5
    source = jnp.clip(source, 0.0, total // factor - 1.0)
    here = col * own_from + first_from + lax.broadcasted_iota(jnp.int32, (width, width_from), 1)
    weight = jnp.maximum(0.0, 1.0 - jnp.abs(source - here.astype(jnp.float32)))
    return jnp.where((place >= 0) & (place < total), weight, 0.0).astype(jnp.bfloat16)


def back(
    sizes, f1, f2, t3, top, lat1, lat2, lat3, smooth, join, offsets, out,
    p3, p2, p1, s3, s2, joint, wide,
):
    count_r, count_c = sizes
    row, col = lax.axis_index("row"), lax.axis_index("col")
    at_top, at_bottom = row == 0, row == count_r - 1
    h1, w1, channels = out.shape
    h2, w2, h3, w3, h4, w4 = h1 // 2, w1 // 2, h1 // 4, w1 // 4, h1 // 8, w1 // 8
    n1, n2, n3 = w1 + 16, w2 + 16, p3.shape[1]
    n4 = top.shape[0] // (h4 + 4)
    pack3 = t3.shape[1] // (h3 + 4)

    def inside(first, width, own):
        place = col * own + first + lax.broadcasted_iota(jnp.int32, (1, width, 1), 1)
        return (place >= 0) & (place < own * count_c)

    def row_inside(t, h):
        if t < 0:
            return jnp.logical_not(at_top)
        if t >= h:
            return jnp.logical_not(at_bottom)
        return None

    def widen(read, matrix, h, border):
        width = matrix.shape[0]
        for r in range(h + 2 * border):
            wide[r, 0:width] = dot(matrix, read(r))

        @pl.when(at_top)
        def _():
            wide[border - 1, 0:width] = wide[border, 0:width]

        @pl.when(at_bottom)
        def _():
            wide[border + h, 0:width] = wide[border + h - 1, 0:width]

    def interpolate(t, factor, border, width):
        source = (t + 0.5) / factor - 0.5
        low = int(np.floor(source))
        weight = float(source - low)
        return (
            wide[border + low, 0:width] * (1.0 - weight)
            + wide[border + low + 1, 0:width] * weight
        )

    def store_row(target, index, value, t, h, lanes=slice(None)):
        keep = row_inside(t, h)
        if keep is not None:
            value = jnp.where(keep, value, 0.0)
        target[index, :, lanes] = value.astype(jnp.bfloat16)

    def taps(read, weight, stride, rows):
        size = rows * stride
        sums = []
        for dx in range(3):
            total = None
            for dy in range(3):
                term = dot(read(dy), weight(dy, dx))
                total = term if total is None else total + term
            sums.append(total)
        return sums[1] + pltpu.roll(sums[0], 1, 0) + pltpu.roll(sums[2], size - 1, 0)

    term = None
    share = t3.shape[2]
    for part in range(count_c):
        piece = dot(t3[part], lat3[part * share : (part + 1) * share])
        term = piece if term is None else term + piece
    term = jnp.maximum(term + offsets[7:8], 0.0).reshape(h3 + 4, pack3, channels)
    term = jnp.concatenate(
        [term, jnp.zeros((h3 + 4, n3 - pack3, channels), jnp.float32)], axis=1
    )
    keep = inside(-4, n3, w3)
    widen(lambda r: top[r * n4 : (r + 1) * n4],
          column_matrix(col, w3, -4, n3, w4, -4, n4, 2, w3 * count_c), h4, 2)
    for t in range(-2, h3 + 2):
        value = jnp.where(keep[0], term[t + 2] + interpolate(t, 2, 2, n3), 0.0)
        store_row(p3, t + 2, value, t, h3)

    term = dot(f2[...].reshape((h2 + 4) * f2.shape[1], f2.shape[2]), lat2[...])
    term = jnp.maximum(term + offsets[6:7], 0.0).reshape(h2 + 4, f2.shape[1], channels)
    keep = inside(-8, n2, w2)
    widen(lambda r: p3[r], column_matrix(col, w2, -8, n2, w3, -4, n3, 2, w2 * count_c), h3, 2)
    for t in range(-2, h2 + 2):
        value = jnp.where(keep[0], term[t + 2, 8 : 8 + n2] + interpolate(t, 2, 2, n2), 0.0)
        store_row(p2, t + 2, value, t, h2)

    keep = inside(-8, n1, w1)
    widen(lambda r: p2[r], column_matrix(col, w1, -8, n1, w2, -8, n2, 2, w1 * count_c), h2, 2)
    for t in range(-2, h1 + 2):
        term = jnp.maximum(dot(f1[t + 2], lat1[...]) + offsets[5:6], 0.0)
        value = jnp.where(keep[0], term[8 : 8 + n1] + interpolate(t, 2, 2, n1), 0.0)
        store_row(p1, t + 2, value, t, h1)

    value = taps(lambda dy: p3[dy : dy + h3 + 2].reshape((h3 + 2) * n3, channels),
                 lambda dy, dx: smooth[2, dy, dx], n3, h3 + 2)
    s3[...] = jnp.maximum(value + offsets[10:11], 0.0).astype(jnp.bfloat16).reshape(s3.shape)
    value = taps(lambda dy: p2[dy : dy + h2 + 2].reshape((h2 + 2) * n2, channels),
                 lambda dy, dx: smooth[1, dy, dx], n2, h2 + 2)
    s2[...] = jnp.maximum(value + offsets[9:10], 0.0).astype(jnp.bfloat16).reshape(s2.shape)

    group = 6
    @pl.loop(0, (h1 + 2) // group)
    def _(block):
        value = taps(
            lambda dy: p1[pl.ds(block * group + dy, group)].reshape(group * n1, channels),
            lambda dy, dx: smooth[0, dy, dx], n1, group,
        )
        value = jnp.maximum(value + offsets[8:9], 0.0).reshape(group, n1, channels)
        value = jnp.where(keep, value, 0.0)
        joint[pl.ds(block * group, group), :, 0:channels] = value.astype(jnp.bfloat16)

    @pl.when(at_top)
    def _():
        joint[0, :, 0:channels] = jnp.zeros((n1, channels), jnp.bfloat16)

    @pl.when(at_bottom)
    def _():
        joint[h1 + 1, :, 0:channels] = jnp.zeros((n1, channels), jnp.bfloat16)

    total1 = w1 * count_c
    for number, (read, matrix, factor, h, border) in enumerate((
        (lambda r: s2[r], column_matrix(col, w1, -8, n1, w2, -8, n2, 2, total1), 2, h2, 1),
        (lambda r: s3[r], column_matrix(col, w1, -8, n1, w3, -4, n3, 4, total1), 4, h3, 1),
        (lambda r: top[r * n4 : (r + 1) * n4],
         column_matrix(col, w1, -8, n1, w4, -4, n4, 8, total1), 8, h4, 2),
    )):
        widen(read, matrix, h, border)
        lanes = slice((number + 1) * channels, (number + 2) * channels)
        for t in range(-1, h1 + 1):
            store_row(joint, t + 1, interpolate(t, factor, border, n1), t, h1, lanes)

    rows = 4
    @pl.loop(0, h1 // rows)
    def _(block):
        value = taps(
            lambda dy: joint[pl.ds(block * rows + dy, rows)].reshape(rows * n1, joint.shape[2]),
            lambda dy, dx: join[dy, dx], n1, rows,
        )
        value = jnp.maximum(value + offsets[11:12], 0.0).reshape(rows, n1, channels)
        out[pl.ds(block * rows, rows)] = value[:, 8 : 8 + w1].astype(jnp.bfloat16)


def local(
    sizes, level_one, level_two, level_three, level_four, bin_weight, neck_feature, neck_pooled,
    lateral_one, lateral_two, lateral_three, smooth_weight, join_weight, biases,
):
    count_r, count_c = sizes
    h1, w1, c1 = level_one.shape
    h2, w2, c2 = level_two.shape
    h3, wide3, c3 = level_three.shape
    h4, wide4, c4 = level_four.shape
    channels = bin_weight.shape[2]
    share = neck_pooled.shape[2]
    w3, w4 = wide3 // count_c, wide4 // count_c
    bf16, f32 = jnp.bfloat16, jnp.float32
    grid_rows = h4 * count_r
    member, scale = pool_counts(grid_rows, wide4)
    spread = spread_table(grid_rows, wide4, 3)
    pack3, pack4 = w3 + 8, w4 + 8
    pick_top = pick_table(h4 + 4, wide4, count_c, -4, pack4)
    pick_three = pick_table(h3 + 4, wide3, count_c, -4, pack3)
    vmem = pl.BlockSpec(memory_space=pltpu.VMEM)
    dma = pltpu.SemaphoreType.DMA
    frames = pl.pallas_call(
        functools.partial(front, sizes),
        out_shape=(
            jax.ShapeDtypeStruct((h1 + 4, w1 + 2 * EDGE, c1), bf16),
            jax.ShapeDtypeStruct((h2 + 4, w2 + 2 * EDGE, c2), bf16),
            jax.ShapeDtypeStruct((count_c, (h3 + 4) * pack3, c3), bf16),
            jax.ShapeDtypeStruct(((h4 + 4) * pack4, channels), bf16),
        ),
        in_specs=[vmem] * 14,
        out_specs=[vmem] * 4,
        scratch_shapes=[
            pltpu.VMEM((grid_rows + 6, wide4, c4), bf16),
            pltpu.VMEM((h3 + 4, wide3, c3), bf16),
            pltpu.VMEM((count_c, (h3 + 4) * pack3, c3), bf16),
            pltpu.VMEM((count_c, CELLS, share), bf16),
            pltpu.VMEM((count_c, CELLS, share), bf16),
            pltpu.VMEM((count_c, (h4 + 4) * pack4, channels), bf16),
            pltpu.VMEM((count_c, (h4 + 4) * pack4, channels), bf16),
            pltpu.VMEM((h4 + 6, wide4, share), bf16),
            dma((2, max(count_r - 1, 1))),
            dma((2, 6)),
            dma((2, 4)),
            dma((2, max(count_c - 1, 1))),
            dma((2, max(count_c - 1, 1))),
            dma((2, max(count_c - 1, 1))),
        ],
        compiler_params=pltpu.CompilerParams(
            collective_id=0, has_side_effects=True, vmem_limit_bytes=48 * 1024 * 1024
        ),
        name="front",
    )(
        level_one, level_two, level_three, level_four, bin_weight, neck_feature, neck_pooled,
        biases, biases[: len(bin_sides)].reshape(-1, share),
        jnp.asarray(member, bf16), jnp.asarray(scale), jnp.asarray(spread),
        jnp.asarray(pick_top, bf16), jnp.asarray(pick_three, bf16),
    )
    n1, n2, n3 = w1 + 16, w2 + 16, round_up(pack3, 16)
    return pl.pallas_call(
        functools.partial(back, sizes),
        out_shape=jax.ShapeDtypeStruct((h1, w1, channels), bf16),
        in_specs=[vmem] * 10,
        out_specs=vmem,
        scratch_shapes=[
            pltpu.VMEM((h3 + 4, n3, channels), bf16),
            pltpu.VMEM((h2 + 4, n2, channels), bf16),
            pltpu.VMEM((h1 + 4, n1, channels), bf16),
            pltpu.VMEM((h3 + 2, n3, channels), bf16),
            pltpu.VMEM((h2 + 2, n2, channels), bf16),
            pltpu.VMEM((h1 + 2, n1, 4 * channels), bf16),
            pltpu.VMEM((h2 + 4, n1, channels), f32),
        ],
        compiler_params=pltpu.CompilerParams(vmem_limit_bytes=56 * 1024 * 1024),
        name="back",
    )(*frames, lateral_one, lateral_two, lateral_three, smooth_weight, join_weight, biases)


def solution(mesh):
    placed = (
        P(("grp", "row"), "col", None),
        P(("grp", "row"), "col", None),
        P(("grp", "row"), None, "col"),
        P(("grp", "row"), None, "col"),
        P(None, "col", None),
        P(None, None, "col", None),
        P(None, None, "col", None),
        P(),
        P(),
        P(),
        P(),
        P(),
        P(),
    )
    sizes = (mesh.shape["row"], mesh.shape["col"])
    return jax.shard_map(
        functools.partial(local, sizes), mesh=mesh, in_specs=placed,
        out_specs=P(("grp", "row"), "col", None), check_vma=False,
    )
```

```python
import functools
import jax
import jax.numpy as jnp
import numpy as np
from jax import lax
from jax.experimental import pallas as pl
from jax.experimental.pallas import tpu as pltpu
from jax.sharding import PartitionSpec as P

bin_sides = (1, 2, 3, 6)
MESH = pl.DeviceIdType.MESH
EDGE = 16
CELLS = 48


def round_up(value, unit):
    return -(-value // unit) * unit


def pool_counts(rows, cols):
    member = np.zeros((len(bin_sides) * CELLS, rows * cols), np.float32)
    scale = np.zeros((len(bin_sides) * CELLS, 1), np.float32)
    for k, b in enumerate(bin_sides):
        for i in range(b):
            for j in range(b):
                r0, r1 = i * rows // b, -(-(i + 1) * rows // b)
                c0, c1 = j * cols // b, -(-(j + 1) * cols // b)
                cell = np.zeros((rows, cols), np.float32)
                cell[r0:r1, c0:c1] = 1.0
                member[k * CELLS + i * b + j] = cell.reshape(-1)
                scale[k * CELLS + i * b + j] = 1.0 / ((r1 - r0) * (c1 - c0))
    return member, scale


def stretch(count, bin_side):
    place = np.arange(count, dtype=np.float32)
    source = np.clip((place + 0.5) * bin_side / count - 0.5, 0.0, bin_side - 1.0)
    return np.maximum(0.0, 1.0 - np.abs(source[:, None] - np.arange(bin_side)[None, :]))


def spread_table(rows, cols, border):
    table = np.zeros((len(bin_sides), rows + 2 * border, cols, CELLS), np.float32)
    for k, b in enumerate(bin_sides):
        both = stretch(rows, b)[:, None, :, None] * stretch(cols, b)[None, :, None, :]
        table[k, border : border + rows, :, : b * b] = both.reshape(rows, cols, b * b)
    return table.reshape(len(bin_sides), (rows + 2 * border) * cols, CELLS)


def pick_table(rows, cols, parts, first, width):
    own = cols // parts
    table = np.zeros((parts, rows, width, rows, cols), np.float32)
    for part in range(parts):
        for j in range(width):
            source = part * own + first + j
            if 0 <= source < cols:
                for r in range(rows):
                    table[part, r, j, r, source] = 1.0
    return table.reshape(parts * rows * width, rows * cols)


def dot(a, b):
    return jnp.dot(a, b, preferred_element_type=jnp.float32)


def column_pick(height, count, base, flip):
    shape = (height * EDGE, count) if flip else (count, height * EDGE)
    packed = lax.broadcasted_iota(jnp.int32, shape, 1 if flip else 0)
    place = lax.broadcasted_iota(jnp.int32, shape, 0 if flip else 1)
    hit = place == lax.div(packed, 2) * EDGE + base + lax.rem(packed, 2)
    return jnp.where(hit, 1.0, 0.0).astype(jnp.bfloat16)


def front(
    sizes, one_h, two_h, three_h, four_h, bins_h, neck_h, necked_h, offsets_h, member_h, scale_h,
    spread_h, pick_top_h, pick_three_h,
    f1, f2, t3, top,
    three, bins, neck, necked, offsets, member, scale, table, pick_top, pick_three,
    grid, send3, bin_out, bin_in, sendt, gott, ppm, out1, in1, out2, in2,
    sem_local, sem_four, sem_row, sem_col, sem_three, sem_bin, sem_top,
):
    count_r, count_c = sizes
    row, col = lax.axis_index("row"), lax.axis_index("col")
    h1, w1, _ = one_h.shape
    h2, w2, _ = two_h.shape
    h3, w3, _ = three.shape
    h4, w4, c4 = four_h.shape
    share = necked.shape[2]
    channels = neck.shape[3]
    packed_row = t3.shape[1] // (h3 + 4)
    halo3, own3 = 2 * packed_row, h3 * packed_row
    wide_t = top.shape[0]
    border = 3
    tall = h4 + 4
    branch = col * share // channels

    def fetch(source, target, number):
        copy = pltpu.make_async_copy(source, target, sem_local.at[number])
        copy.start()
        return copy

    get_three = [fetch(three_h, three, 0), fetch(pick_three_h, pick_three, 1)]
    get_four = [
        fetch(four_h, grid.at[pl.ds(border + row * h4, h4)], 2), fetch(member_h, member, 3),
        fetch(scale_h, scale, 4), fetch(bins_h, bins, 5),
    ]
    get_one = [
        fetch(one_h, f1.at[2 : 2 + h1, EDGE : EDGE + w1], 6),
        fetch(two_h, f2.at[2 : 2 + h2, EDGE : EDGE + w2], 7),
    ]
    get_neck = [fetch(neck_h, neck, 8)]
    get_rest = [
        fetch(spread_h.at[branch, pl.ds(row * h4 * w4, (tall + 2) * w4)], table, 9),
        fetch(offsets_h, offsets, 10), fetch(necked_h, necked, 11), fetch(pick_top_h, pick_top, 12),
    ]

    for frame, h in ((f1, h1), (f2, h2)):
        rim = jnp.zeros((2, frame.shape[1], frame.shape[2]), frame.dtype)
        frame[0:2] = rim
        frame[2 + h :] = rim
    in1[...] = jnp.zeros(in1.shape, in1.dtype)
    in2[...] = jnp.zeros(in2.shape, in2.dtype)
    rim = jnp.zeros((count_c, halo3, t3.shape[2]), t3.dtype)
    t3[:, 0:halo3] = rim
    t3[:, halo3 + own3 :] = rim
    grid[0:border] = jnp.zeros((border, w4, c4), grid.dtype)
    grid[border + h4 * count_r :] = jnp.zeros((border, w4, c4), grid.dtype)

    barrier = pltpu.get_barrier_semaphore()
    for step in range(1, count_r):
        pl.semaphore_signal(
            barrier, inc=1, device_id={"row": lax.rem(row + step, count_r)}, device_id_type=MESH
        )
    for step in range(1, count_c):
        pl.semaphore_signal(
            barrier, inc=1, device_id={"col": lax.rem(col + step, count_c)}, device_id_type=MESH
        )
    pl.semaphore_wait(barrier, count_r + count_c - 2)

    def remote(source, target, sems, number, where):
        return pltpu.make_async_remote_copy(
            src_ref=source, dst_ref=target, send_sem=sems.at[0, number],
            recv_sem=sems.at[1, number], device_id=where, device_id_type=MESH,
        )

    def when_each(condition, copies, act):
        @pl.when(condition)
        def _():
            for copy in copies:
                getattr(copy, act)()

    has_up, has_down = row > 0, row < count_r - 1
    has_left, has_right = col > 0, col < count_c - 1

    four_copies = []
    for step in range(1, count_r):
        copy = remote(
            four_h, grid.at[pl.ds(border + row * h4, h4)], sem_four, step - 1,
            {"row": lax.rem(row + step, count_r)},
        )
        copy.start()
        four_copies.append(copy)
    for copy in get_three:
        copy.wait()
    tall3 = three[...].reshape(h3 * w3, three.shape[2])
    three_copies = []
    for part in range(count_c):
        send3[part] = dot(pick_three[part * own3 : (part + 1) * own3], tall3).astype(jnp.bfloat16)
    for step in range(1, count_c):
        there = lax.rem(col + step, count_c)
        copy = remote(
            send3.at[there], t3.at[col, halo3 : halo3 + own3], sem_three, step - 1, {"col": there}
        )
        copy.start()
        three_copies.append(copy)
    t3[pl.ds(col, 1), halo3 : halo3 + own3] = send3[pl.ds(col, 1)]

    up_copies, down_copies = [], []
    for number, (block, frame, h, w) in enumerate(((one_h, f1, h1, w1), (two_h, f2, h2, w2))):
        up_copies.append(
            remote(block.at[0:2], frame.at[2 + h : 4 + h, EDGE : EDGE + w], sem_row, number,
                   {"row": row - 1})
        )
        down_copies.append(
            remote(block.at[h - 2 : h], frame.at[0:2, EDGE : EDGE + w], sem_row, 2 + number,
                   {"row": row + 1})
        )
    when_each(has_up, up_copies, "start")
    when_each(has_down, down_copies, "start")

    for copy in get_four:
        copy.wait()
    for copy in four_copies:
        copy.wait_recv()
    whole = grid[border : border + h4 * count_r].reshape(h4 * count_r * w4, c4)
    pooled = dot(member[...], whole) * scale[...]
    high = pooled.astype(jnp.bfloat16)
    low = (pooled - high.astype(jnp.float32)).astype(jnp.bfloat16)
    pieces = channels // share
    for k in range(len(bin_sides)):
        rows = slice(k * CELLS, (k + 1) * CELLS)
        part = (dot(high[rows], bins[k]) + dot(low[rows], bins[k])).astype(jnp.bfloat16)
        for piece in range(pieces):
            bin_out[k * pieces + piece] = part[:, piece * share : (piece + 1) * share]
    bin_copies = []
    for step in range(1, count_c):
        there = lax.rem(col + step, count_c)
        copy = remote(bin_out.at[there], bin_in.at[col], sem_bin, step - 1, {"col": there})
        copy.start()
        bin_copies.append(copy)
    bin_in[pl.ds(col, 1)] = bin_out[pl.ds(col, 1)]

    for copy in get_neck:
        copy.wait()
    terms = [None] * 3
    for dy in range(3):
        window = grid[pl.ds(row * h4 + dy, tall)].reshape(tall * w4, c4)
        for dx in range(3):
            term = dot(window, neck[dy, dx])
            terms[dx] = term if dy == 0 else terms[dx] + term

    for copy in get_rest:
        copy.wait()
    for copy in bin_copies:
        copy.wait_recv()
    total = bin_in[0].astype(jnp.float32)
    for part in range(1, count_c):
        total = total + bin_in[part].astype(jnp.float32)
    line = offsets[pl.ds(branch, 1)]
    shift = line[:, 0:share]
    for piece in range(1, pieces):
        shift = jnp.where(
            lax.rem(col, pieces) == piece, line[:, piece * share : (piece + 1) * share], shift
        )
    binned = jnp.maximum(total + shift, 0.0)
    ppm[...] = (
        jnp.dot(
            table[...], binned, precision=lax.Precision.HIGHEST, preferred_element_type=jnp.float32
        )
        .astype(jnp.bfloat16)
        .reshape(tall + 2, w4, share)
    )
    for dy in range(3):
        window = ppm[dy : dy + tall].reshape(tall * w4, share)
        for dx in range(3):
            terms[dx] = terms[dx] + dot(window, necked[dy, dx])
    place = lax.rem(lax.broadcasted_iota(jnp.int32, (tall * w4, 1), 0), w4)
    partial = (
        terms[1]
        + jnp.where(place > 0, pltpu.roll(terms[0], 1, 0), 0.0)
        + jnp.where(place < w4 - 1, pltpu.roll(terms[2], tall * w4 - 1, 0), 0.0)
    ).astype(jnp.bfloat16)
    for part in range(count_c):
        sendt[part] = dot(pick_top[part * wide_t : (part + 1) * wide_t], partial).astype(
            jnp.bfloat16
        )
    top_copies = []
    for step in range(1, count_c):
        there = lax.rem(col + step, count_c)
        copy = remote(sendt.at[there], gott.at[col], sem_top, step - 1, {"col": there})
        copy.start()
        top_copies.append(copy)
    gott[pl.ds(col, 1)] = sendt[pl.ds(col, 1)]

    for copy in three_copies:
        copy.wait_recv()
    up3 = remote(t3.at[:, halo3 : 2 * halo3], t3.at[:, halo3 + own3 :], sem_row, 4,
                 {"row": row - 1})
    down3 = remote(t3.at[:, own3 : own3 + halo3], t3.at[:, 0:halo3], sem_row, 5, {"row": row + 1})
    when_each(has_up, [up3], "start")
    when_each(has_down, [down3], "start")
    for copy in get_one:
        copy.wait()
    when_each(has_down, up_copies, "wait_recv")
    when_each(has_up, down_copies, "wait_recv")
    left_copies, right_copies = [], []
    for number, (frame, h, w, outgoing, incoming) in enumerate(
        ((f1, h1 + 4, w1, out1, in1), (f2, h2 + 4, w2, out2, in2))
    ):
        count, depth = outgoing.shape[1:]
        block = frame[:, EDGE : 2 * EDGE].reshape(h * EDGE, depth)
        outgoing[0] = dot(column_pick(h, count, 0, False), block).astype(jnp.bfloat16)
        block = frame[:, w : EDGE + w].reshape(h * EDGE, depth)
        outgoing[1] = dot(column_pick(h, count, EDGE - 2, False), block).astype(jnp.bfloat16)
        left_copies.append(
            remote(outgoing.at[0], incoming.at[1], sem_col, number, {"col": col - 1})
        )
        right_copies.append(
            remote(outgoing.at[1], incoming.at[0], sem_col, 2 + number, {"col": col + 1})
        )
    when_each(has_left, left_copies, "start")
    when_each(has_right, right_copies, "start")

    for copy in top_copies:
        copy.wait_recv()
    total = gott[0].astype(jnp.float32)
    for part in range(1, count_c):
        total = total + gott[part].astype(jnp.float32)
    top[...] = jnp.maximum(total + offsets[4:5], 0.0).astype(jnp.bfloat16)

    when_each(has_right, left_copies, "wait_recv")
    when_each(has_left, right_copies, "wait_recv")
    for frame, h, w, incoming in ((f1, h1 + 4, w1, in1), (f2, h2 + 4, w2, in2)):
        count, depth = incoming.shape[1:]
        value = dot(column_pick(h, count, EDGE - 2, True), incoming[0])
        frame[:, 0:EDGE] = value.astype(jnp.bfloat16).reshape(h, EDGE, depth)
        value = dot(column_pick(h, count, 0, True), incoming[1])
        frame[:, EDGE + w :] = value.astype(jnp.bfloat16).reshape(h, EDGE, depth)
    when_each(has_down, [up3], "wait_recv")
    when_each(has_up, [down3], "wait_recv")

    for copy in four_copies + bin_copies + three_copies + top_copies:
        copy.wait_send()
    when_each(has_up, up_copies + [up3], "wait_send")
    when_each(has_down, down_copies + [down3], "wait_send")
    when_each(has_left, left_copies, "wait_send")
    when_each(has_right, right_copies, "wait_send")


def column_matrix(col, own, first, width, own_from, first_from, width_from, factor, total):
    place = col * own + first + lax.broadcasted_iota(jnp.int32, (width, width_from), 0)
    source = (place.astype(jnp.float32) + 0.5) / factor - 0.5
    source = jnp.clip(source, 0.0, total // factor - 1.0)
    here = col * own_from + first_from + lax.broadcasted_iota(jnp.int32, (width, width_from), 1)
    weight = jnp.maximum(0.0, 1.0 - jnp.abs(source - here.astype(jnp.float32)))
    return jnp.where((place >= 0) & (place < total), weight, 0.0).astype(jnp.bfloat16)


def back(
    sizes, f1_h, f2_h, t3_h, top_h, lat1_h, lat2_h, lat3_h, smooth_h, join_h, offsets_h, out,
    f1, f2, t3, top, lat1, lat2, lat3, smooth, join, offsets, p3, p2, p1, s3, s2, joint, wide, sems,
):
    fetches = []
    for source, target in (
        (t3_h, t3), (lat3_h, lat3), (offsets_h, offsets), (top_h, top), (f2_h, f2), (lat2_h, lat2),
        (f1_h, f1), (lat1_h, lat1), (smooth_h, smooth), (join_h, join),
    ):
        copy = pltpu.make_async_copy(source, target, sems.at[len(fetches)])
        copy.start()
        fetches.append(copy)
    count_r, count_c = sizes
    row, col = lax.axis_index("row"), lax.axis_index("col")
    at_top, at_bottom = row == 0, row == count_r - 1
    h1, w1, channels = out.shape
    h2, w2, h3, w3, h4, w4 = h1 // 2, w1 // 2, h1 // 4, w1 // 4, h1 // 8, w1 // 8
    n1, n2, n3 = w1 + 16, w2 + 16, p3.shape[1]
    n4 = top.shape[0] // (h4 + 4)
    pack3 = t3.shape[1] // (h3 + 4)

    def inside(first, width, own):
        place = col * own + first + lax.broadcasted_iota(jnp.int32, (1, width, 1), 1)
        return (place >= 0) & (place < own * count_c)

    def row_inside(t, h):
        if t < 0:
            return jnp.logical_not(at_top)
        if t >= h:
            return jnp.logical_not(at_bottom)
        return None

    def widen(read, matrix, h, border):
        width = matrix.shape[0]
        for r in range(h + 2 * border):
            wide[r, 0:width] = dot(matrix, read(r))

        @pl.when(at_top)
        def _():
            wide[border - 1, 0:width] = wide[border, 0:width]

        @pl.when(at_bottom)
        def _():
            wide[border + h, 0:width] = wide[border + h - 1, 0:width]

    def interpolate(t, factor, border, width):
        source = (t + 0.5) / factor - 0.5
        low = int(np.floor(source))
        weight = float(source - low)
        return (
            wide[border + low, 0:width] * (1.0 - weight)
            + wide[border + low + 1, 0:width] * weight
        )

    def store_row(target, index, value, t, h, lanes=slice(None)):
        keep = row_inside(t, h)
        if keep is not None:
            value = jnp.where(keep, value, 0.0)
        target[index, :, lanes] = value.astype(jnp.bfloat16)

    def taps(read, weight, stride, rows):
        size = rows * stride
        sums = []
        for dx in range(3):
            total = None
            for dy in range(3):
                term = dot(read(dy), weight(dy, dx))
                total = term if total is None else total + term
            sums.append(total)
        return sums[1] + pltpu.roll(sums[0], 1, 0) + pltpu.roll(sums[2], size - 1, 0)

    for copy in fetches[0:4]:
        copy.wait()
    term = None
    share = t3.shape[2]
    for part in range(count_c):
        piece = dot(t3[part], lat3[part * share : (part + 1) * share])
        term = piece if term is None else term + piece
    term = jnp.maximum(term + offsets[7:8], 0.0).reshape(h3 + 4, pack3, channels)
    term = jnp.concatenate(
        [term, jnp.zeros((h3 + 4, n3 - pack3, channels), jnp.float32)], axis=1
    )
    keep = inside(-4, n3, w3)
    widen(lambda r: top[r * n4 : (r + 1) * n4],
          column_matrix(col, w3, -4, n3, w4, -4, n4, 2, w3 * count_c), h4, 2)
    for t in range(-2, h3 + 2):
        value = jnp.where(keep[0], term[t + 2] + interpolate(t, 2, 2, n3), 0.0)
        store_row(p3, t + 2, value, t, h3)

    for copy in fetches[4:6]:
        copy.wait()
    term = dot(f2[...].reshape((h2 + 4) * f2.shape[1], f2.shape[2]), lat2[...])
    term = jnp.maximum(term + offsets[6:7], 0.0).reshape(h2 + 4, f2.shape[1], channels)
    keep = inside(-8, n2, w2)
    widen(lambda r: p3[r], column_matrix(col, w2, -8, n2, w3, -4, n3, 2, w2 * count_c), h3, 2)
    for t in range(-2, h2 + 2):
        value = jnp.where(keep[0], term[t + 2, 8 : 8 + n2] + interpolate(t, 2, 2, n2), 0.0)
        store_row(p2, t + 2, value, t, h2)

    for copy in fetches[6:8]:
        copy.wait()
    keep = inside(-8, n1, w1)
    widen(lambda r: p2[r], column_matrix(col, w1, -8, n1, w2, -8, n2, 2, w1 * count_c), h2, 2)
    for t in range(-2, h1 + 2):
        term = jnp.maximum(dot(f1[t + 2], lat1[...]) + offsets[5:6], 0.0)
        value = jnp.where(keep[0], term[8 : 8 + n1] + interpolate(t, 2, 2, n1), 0.0)
        store_row(p1, t + 2, value, t, h1)

    fetches[8].wait()
    value = taps(lambda dy: p3[dy : dy + h3 + 2].reshape((h3 + 2) * n3, channels),
                 lambda dy, dx: smooth[2, dy, dx], n3, h3 + 2)
    s3[...] = jnp.maximum(value + offsets[10:11], 0.0).astype(jnp.bfloat16).reshape(s3.shape)
    value = taps(lambda dy: p2[dy : dy + h2 + 2].reshape((h2 + 2) * n2, channels),
                 lambda dy, dx: smooth[1, dy, dx], n2, h2 + 2)
    s2[...] = jnp.maximum(value + offsets[9:10], 0.0).astype(jnp.bfloat16).reshape(s2.shape)

    group = 6
    @pl.loop(0, (h1 + 2) // group)
    def _(block):
        value = taps(
            lambda dy: p1[pl.ds(block * group + dy, group)].reshape(group * n1, channels),
            lambda dy, dx: smooth[0, dy, dx], n1, group,
        )
        value = jnp.maximum(value + offsets[8:9], 0.0).reshape(group, n1, channels)
        value = jnp.where(keep, value, 0.0)
        joint[pl.ds(block * group, group), :, 0:channels] = value.astype(jnp.bfloat16)

    @pl.when(at_top)
    def _():
        joint[0, :, 0:channels] = jnp.zeros((n1, channels), jnp.bfloat16)

    @pl.when(at_bottom)
    def _():
        joint[h1 + 1, :, 0:channels] = jnp.zeros((n1, channels), jnp.bfloat16)

    total1 = w1 * count_c
    for number, (read, matrix, factor, h, border) in enumerate((
        (lambda r: s2[r], column_matrix(col, w1, -8, n1, w2, -8, n2, 2, total1), 2, h2, 1),
        (lambda r: s3[r], column_matrix(col, w1, -8, n1, w3, -4, n3, 4, total1), 4, h3, 1),
        (lambda r: top[r * n4 : (r + 1) * n4],
         column_matrix(col, w1, -8, n1, w4, -4, n4, 8, total1), 8, h4, 2),
    )):
        widen(read, matrix, h, border)
        lanes = slice((number + 1) * channels, (number + 2) * channels)
        for t in range(-1, h1 + 1):
            store_row(joint, t + 1, interpolate(t, factor, border, n1), t, h1, lanes)

    fetches[9].wait()
    rows = 4
    @pl.loop(0, h1 // rows)
    def _(block):
        value = taps(
            lambda dy: joint[pl.ds(block * rows + dy, rows)].reshape(rows * n1, joint.shape[2]),
            lambda dy, dx: join[dy, dx], n1, rows,
        )
        value = jnp.maximum(value + offsets[11:12], 0.0).reshape(rows, n1, channels)
        out[pl.ds(block * rows, rows)] = value[:, 8 : 8 + w1].astype(jnp.bfloat16)


def local(
    sizes, level_one, level_two, level_three, level_four, bin_weight, neck_feature, neck_pooled,
    lateral_one, lateral_two, lateral_three, smooth_weight, join_weight, biases,
):
    count_r, count_c = sizes
    h1, w1, c1 = level_one.shape
    h2, w2, c2 = level_two.shape
    h3, wide3, c3 = level_three.shape
    h4, wide4, c4 = level_four.shape
    channels = bin_weight.shape[2]
    share = neck_pooled.shape[2]
    w3, w4 = wide3 // count_c, wide4 // count_c
    bf16, f32 = jnp.bfloat16, jnp.float32
    grid_rows = h4 * count_r
    member, scale = pool_counts(grid_rows, wide4)
    spread = spread_table(grid_rows, wide4, 3)
    pack3, pack4 = w3 + 8, w4 + 8
    pick_top = pick_table(h4 + 4, wide4, count_c, -4, pack4)
    pick_three = pick_table(h3, wide3, count_c, -4, pack3)
    vmem = pl.BlockSpec(memory_space=pltpu.VMEM)
    hbm = pl.BlockSpec(memory_space=pltpu.HBM)
    dma = pltpu.SemaphoreType.DMA
    steps_r, steps_c = max(count_r - 1, 1), max(count_c - 1, 1)
    column1, column2 = round_up(2 * (h1 + 4), 16), round_up(2 * (h2 + 4), 16)
    frames = pl.pallas_call(
        functools.partial(front, sizes),
        out_shape=(
            jax.ShapeDtypeStruct((h1 + 4, w1 + 2 * EDGE, c1), bf16),
            jax.ShapeDtypeStruct((h2 + 4, w2 + 2 * EDGE, c2), bf16),
            jax.ShapeDtypeStruct((count_c, (h3 + 4) * pack3, c3), bf16),
            jax.ShapeDtypeStruct(((h4 + 4) * pack4, channels), bf16),
        ),
        in_specs=[hbm] * 13,
        out_specs=[vmem] * 4,
        scratch_shapes=[
            pltpu.VMEM(level_three.shape, bf16),
            pltpu.VMEM(bin_weight.shape, bf16),
            pltpu.VMEM(neck_feature.shape, bf16),
            pltpu.VMEM(neck_pooled.shape, bf16),
            pltpu.VMEM(biases.shape, f32),
            pltpu.VMEM(member.shape, bf16),
            pltpu.VMEM(scale.shape, f32),
            pltpu.VMEM(((h4 + 6) * wide4, CELLS), f32),
            pltpu.VMEM(pick_top.shape, bf16),
            pltpu.VMEM(pick_three.shape, bf16),
            pltpu.VMEM((grid_rows + 6, wide4, c4), bf16),
            pltpu.VMEM((count_c, h3 * pack3, c3), bf16),
            pltpu.VMEM((count_c, CELLS, share), bf16),
            pltpu.VMEM((count_c, CELLS, share), bf16),
            pltpu.VMEM((count_c, (h4 + 4) * pack4, channels), bf16),
            pltpu.VMEM((count_c, (h4 + 4) * pack4, channels), bf16),
            pltpu.VMEM((h4 + 6, wide4, share), bf16),
            pltpu.VMEM((2, column1, c1), bf16),
            pltpu.VMEM((2, column1, c1), bf16),
            pltpu.VMEM((2, column2, c2), bf16),
            pltpu.VMEM((2, column2, c2), bf16),
            dma((13,)),
            dma((2, steps_r)),
            dma((2, 6)),
            dma((2, 4)),
            dma((2, steps_c)),
            dma((2, steps_c)),
            dma((2, steps_c)),
        ],
        compiler_params=pltpu.CompilerParams(
            collective_id=0, has_side_effects=True, vmem_limit_bytes=60 * 1024 * 1024
        ),
        name="front",
    )(
        level_one, level_two, level_three, level_four, bin_weight, neck_feature, neck_pooled,
        biases, jnp.asarray(member, bf16), jnp.asarray(scale), jnp.asarray(spread),
        jnp.asarray(pick_top, bf16), jnp.asarray(pick_three, bf16),
    )
    n1, n2, n3 = w1 + 16, w2 + 16, round_up(pack3, 16)
    return pl.pallas_call(
        functools.partial(back, sizes),
        out_shape=jax.ShapeDtypeStruct((h1, w1, channels), bf16),
        in_specs=[hbm] * 10,
        out_specs=vmem,
        scratch_shapes=[pltpu.VMEM(frame.shape, bf16) for frame in frames] + [
            pltpu.VMEM(lateral_one.shape, bf16),
            pltpu.VMEM(lateral_two.shape, bf16),
            pltpu.VMEM(lateral_three.shape, bf16),
            pltpu.VMEM(smooth_weight.shape, bf16),
            pltpu.VMEM(join_weight.shape, bf16),
            pltpu.VMEM(biases.shape, f32),
            pltpu.VMEM((h3 + 4, n3, channels), bf16),
            pltpu.VMEM((h2 + 4, n2, channels), bf16),
            pltpu.VMEM((h1 + 4, n1, channels), bf16),
            pltpu.VMEM((h3 + 2, n3, channels), bf16),
            pltpu.VMEM((h2 + 2, n2, channels), bf16),
            pltpu.VMEM((h1 + 2, n1, 4 * channels), bf16),
            pltpu.VMEM((h2 + 4, n1, channels), f32),
            dma((10,)),
        ],
        compiler_params=pltpu.CompilerParams(vmem_limit_bytes=60 * 1024 * 1024),
        name="back",
    )(*frames, lateral_one, lateral_two, lateral_three, smooth_weight, join_weight, biases)


def solution(mesh):
    placed = (
        P(("grp", "row"), "col", None),
        P(("grp", "row"), "col", None),
        P(("grp", "row"), None, "col"),
        P(("grp", "row"), None, "col"),
        P(None, "col", None),
        P(None, None, "col", None),
        P(None, None, "col", None),
        P(),
        P(),
        P(),
        P(),
        P(),
        P(),
    )
    sizes = (mesh.shape["row"], mesh.shape["col"])
    return jax.shard_map(
        functools.partial(local, sizes), mesh=mesh, in_specs=placed,
        out_specs=P(("grp", "row"), "col", None), check_vma=False,
    )
```

```python
import functools
import jax
import jax.numpy as jnp
import numpy as np
from jax import lax
from jax.experimental import pallas as pl
from jax.experimental.pallas import tpu as pltpu
from jax.sharding import PartitionSpec as P

bin_sides = (1, 2, 3, 6)
MESH = pl.DeviceIdType.MESH
EDGE = 16
CELLS = 48


def round_up(value, unit):
    return -(-value // unit) * unit


def pool_counts(rows, cols):
    member = np.zeros((len(bin_sides) * CELLS, rows * cols), np.float32)
    scale = np.zeros((len(bin_sides) * CELLS, 1), np.float32)
    for k, b in enumerate(bin_sides):
        for i in range(b):
            for j in range(b):
                r0, r1 = i * rows // b, -(-(i + 1) * rows // b)
                c0, c1 = j * cols // b, -(-(j + 1) * cols // b)
                cell = np.zeros((rows, cols), np.float32)
                cell[r0:r1, c0:c1] = 1.0
                member[k * CELLS + i * b + j] = cell.reshape(-1)
                scale[k * CELLS + i * b + j] = 1.0 / ((r1 - r0) * (c1 - c0))
    return member, scale


def stretch(count, bin_side):
    place = np.arange(count, dtype=np.float32)
    source = np.clip((place + 0.5) * bin_side / count - 0.5, 0.0, bin_side - 1.0)
    return np.maximum(0.0, 1.0 - np.abs(source[:, None] - np.arange(bin_side)[None, :]))


def spread_table(rows, cols, border):
    table = np.zeros((len(bin_sides), rows + 2 * border, cols, CELLS), np.float32)
    for k, b in enumerate(bin_sides):
        both = stretch(rows, b)[:, None, :, None] * stretch(cols, b)[None, :, None, :]
        table[k, border : border + rows, :, : b * b] = both.reshape(rows, cols, b * b)
    return table.reshape(len(bin_sides), (rows + 2 * border) * cols, CELLS)


def pick_table(rows, cols, parts, first, width):
    own = cols // parts
    table = np.zeros((parts, rows, width, rows, cols), np.float32)
    for part in range(parts):
        for j in range(width):
            source = part * own + first + j
            if 0 <= source < cols:
                for r in range(rows):
                    table[part, r, j, r, source] = 1.0
    return table.reshape(parts * rows * width, rows * cols)


def dot(a, b):
    return jnp.dot(a, b, preferred_element_type=jnp.float32)


def column_pick(height, count, base, flip):
    shape = (height * EDGE, count) if flip else (count, height * EDGE)
    packed = lax.broadcasted_iota(jnp.int32, shape, 1 if flip else 0)
    place = lax.broadcasted_iota(jnp.int32, shape, 0 if flip else 1)
    hit = place == lax.div(packed, 2) * EDGE + base + lax.rem(packed, 2)
    return jnp.where(hit, 1.0, 0.0).astype(jnp.bfloat16)


def front(
    sizes, one_h, two_h, three_h, four_h, bins_h, neck_h, necked_h, offsets_h, member_h, scale_h,
    spread_h, pick_top_h, pick_three_h,
    f1, f2, t3, top,
    three, bins, neck, necked, offsets, member, scale, table, pick_top, pick_three,
    grid, send3, bin_out, bin_in, sendt, gott, ppm, out1, in1, out2, in2,
    sem_local, sem_four, sem_row, sem_col, sem_three, sem_bin, sem_top,
    early, later,
):
    count_r, count_c = sizes
    row, col = lax.axis_index("row"), lax.axis_index("col")
    h1, w1, _ = one_h.shape
    h2, w2, _ = two_h.shape
    h3, w3, _ = three.shape
    h4, w4, c4 = four_h.shape
    share = necked.shape[2]
    channels = neck.shape[3]
    packed_row = t3.shape[1] // (h3 + 4)
    halo3, own3 = 2 * packed_row, h3 * packed_row
    wide_t = top.shape[0]
    border = 3
    tall = h4 + 4
    branch = col * share // channels

    def fetch(source, target, number):
        copy = pltpu.make_async_copy(source, target, sem_local.at[number])
        copy.start()
        return copy

    get_three = [fetch(three_h, three, 0), fetch(pick_three_h, pick_three, 1)]
    get_four = [
        fetch(four_h, grid.at[pl.ds(border + row * h4, h4)], 2), fetch(member_h, member, 3),
        fetch(scale_h, scale, 4), fetch(bins_h, bins, 5),
    ]
    get_one = [
        fetch(one_h, f1.at[2 : 2 + h1, EDGE : EDGE + w1], 6),
        fetch(two_h, f2.at[2 : 2 + h2, EDGE : EDGE + w2], 7),
    ]
    get_neck = [fetch(neck_h, neck, 8)]
    get_rest = [
        fetch(spread_h.at[branch, pl.ds(row * h4 * w4, (tall + 2) * w4)], table, 9),
        fetch(offsets_h, offsets, 10), fetch(necked_h, necked, 11), fetch(pick_top_h, pick_top, 12),
    ]

    early()

    for frame, h in ((f1, h1), (f2, h2)):
        rim = jnp.zeros((2, frame.shape[1], frame.shape[2]), frame.dtype)
        frame[0:2] = rim
        frame[2 + h :] = rim
    in1[...] = jnp.zeros(in1.shape, in1.dtype)
    in2[...] = jnp.zeros(in2.shape, in2.dtype)
    rim = jnp.zeros((count_c, halo3, t3.shape[2]), t3.dtype)
    t3[:, 0:halo3] = rim
    t3[:, halo3 + own3 :] = rim
    grid[0:border] = jnp.zeros((border, w4, c4), grid.dtype)
    grid[border + h4 * count_r :] = jnp.zeros((border, w4, c4), grid.dtype)

    barrier = pltpu.get_barrier_semaphore()
    for step in range(1, count_r):
        pl.semaphore_signal(
            barrier, inc=1, device_id={"row": lax.rem(row + step, count_r)}, device_id_type=MESH
        )
    for step in range(1, count_c):
        pl.semaphore_signal(
            barrier, inc=1, device_id={"col": lax.rem(col + step, count_c)}, device_id_type=MESH
        )
    pl.semaphore_wait(barrier, count_r + count_c - 2)

    def remote(source, target, sems, number, where):
        return pltpu.make_async_remote_copy(
            src_ref=source, dst_ref=target, send_sem=sems.at[0, number],
            recv_sem=sems.at[1, number], device_id=where, device_id_type=MESH,
        )

    def when_each(condition, copies, act):
        @pl.when(condition)
        def _():
            for copy in copies:
                getattr(copy, act)()

    has_up, has_down = row > 0, row < count_r - 1
    has_left, has_right = col > 0, col < count_c - 1

    four_copies = []
    for step in range(1, count_r):
        copy = remote(
            four_h, grid.at[pl.ds(border + row * h4, h4)], sem_four, step - 1,
            {"row": lax.rem(row + step, count_r)},
        )
        copy.start()
        four_copies.append(copy)
    for copy in get_three:
        copy.wait()
    tall3 = three[...].reshape(h3 * w3, three.shape[2])
    three_copies = []
    for part in range(count_c):
        send3[part] = dot(pick_three[part * own3 : (part + 1) * own3], tall3).astype(jnp.bfloat16)
    for step in range(1, count_c):
        there = lax.rem(col + step, count_c)
        copy = remote(
            send3.at[there], t3.at[col, halo3 : halo3 + own3], sem_three, step - 1, {"col": there}
        )
        copy.start()
        three_copies.append(copy)
    t3[pl.ds(col, 1), halo3 : halo3 + own3] = send3[pl.ds(col, 1)]

    up_copies, down_copies = [], []
    for number, (block, frame, h, w) in enumerate(((one_h, f1, h1, w1), (two_h, f2, h2, w2))):
        up_copies.append(
            remote(block.at[0:2], frame.at[2 + h : 4 + h, EDGE : EDGE + w], sem_row, number,
                   {"row": row - 1})
        )
        down_copies.append(
            remote(block.at[h - 2 : h], frame.at[0:2, EDGE : EDGE + w], sem_row, 2 + number,
                   {"row": row + 1})
        )
    when_each(has_up, up_copies, "start")
    when_each(has_down, down_copies, "start")

    for copy in get_four:
        copy.wait()
    for copy in four_copies:
        copy.wait_recv()
    whole = grid[border : border + h4 * count_r].reshape(h4 * count_r * w4, c4)
    pooled = dot(member[...], whole) * scale[...]
    high = pooled.astype(jnp.bfloat16)
    low = (pooled - high.astype(jnp.float32)).astype(jnp.bfloat16)
    pieces = channels // share
    for k in range(len(bin_sides)):
        rows = slice(k * CELLS, (k + 1) * CELLS)
        part = (dot(high[rows], bins[k]) + dot(low[rows], bins[k])).astype(jnp.bfloat16)
        for piece in range(pieces):
            bin_out[k * pieces + piece] = part[:, piece * share : (piece + 1) * share]
    bin_copies = []
    for step in range(1, count_c):
        there = lax.rem(col + step, count_c)
        copy = remote(bin_out.at[there], bin_in.at[col], sem_bin, step - 1, {"col": there})
        copy.start()
        bin_copies.append(copy)
    bin_in[pl.ds(col, 1)] = bin_out[pl.ds(col, 1)]

    for copy in get_one:
        copy.wait()
    when_each(has_down, up_copies, "wait_recv")
    when_each(has_up, down_copies, "wait_recv")
    left_copies, right_copies = [], []
    for number, (frame, h, w, outgoing, incoming) in enumerate(
        ((f1, h1 + 4, w1, out1, in1), (f2, h2 + 4, w2, out2, in2))
    ):
        count, depth = outgoing.shape[1:]
        block = frame[:, EDGE : 2 * EDGE].reshape(h * EDGE, depth)
        outgoing[0] = dot(column_pick(h, count, 0, False), block).astype(jnp.bfloat16)
        block = frame[:, w : EDGE + w].reshape(h * EDGE, depth)
        outgoing[1] = dot(column_pick(h, count, EDGE - 2, False), block).astype(jnp.bfloat16)
        left_copies.append(
            remote(outgoing.at[0], incoming.at[1], sem_col, number, {"col": col - 1})
        )
        right_copies.append(
            remote(outgoing.at[1], incoming.at[0], sem_col, 2 + number, {"col": col + 1})
        )
    when_each(has_left, left_copies, "start")
    when_each(has_right, right_copies, "start")

    for copy in get_neck:
        copy.wait()
    terms = [None] * 3
    for dy in range(3):
        window = grid[pl.ds(row * h4 + dy, tall)].reshape(tall * w4, c4)
        for dx in range(3):
            term = dot(window, neck[dy, dx])
            terms[dx] = term if dy == 0 else terms[dx] + term

    for copy in three_copies:
        copy.wait_recv()
    up3 = remote(t3.at[:, halo3 : 2 * halo3], t3.at[:, halo3 + own3 :], sem_row, 4,
                 {"row": row - 1})
    down3 = remote(t3.at[:, own3 : own3 + halo3], t3.at[:, 0:halo3], sem_row, 5, {"row": row + 1})
    when_each(has_up, [up3], "start")
    when_each(has_down, [down3], "start")

    for copy in get_rest:
        copy.wait()
    for copy in bin_copies:
        copy.wait_recv()
    total = bin_in[0].astype(jnp.float32)
    for part in range(1, count_c):
        total = total + bin_in[part].astype(jnp.float32)
    line = offsets[pl.ds(branch, 1)]
    shift = line[:, 0:share]
    for piece in range(1, pieces):
        shift = jnp.where(
            lax.rem(col, pieces) == piece, line[:, piece * share : (piece + 1) * share], shift
        )
    binned = jnp.maximum(total + shift, 0.0)
    ppm[...] = (
        jnp.dot(
            table[...], binned, precision=lax.Precision.HIGHEST, preferred_element_type=jnp.float32
        )
        .astype(jnp.bfloat16)
        .reshape(tall + 2, w4, share)
    )
    for dy in range(3):
        window = ppm[dy : dy + tall].reshape(tall * w4, share)
        for dx in range(3):
            terms[dx] = terms[dx] + dot(window, necked[dy, dx])
    place = lax.rem(lax.broadcasted_iota(jnp.int32, (tall * w4, 1), 0), w4)
    partial = (
        terms[1]
        + jnp.where(place > 0, pltpu.roll(terms[0], 1, 0), 0.0)
        + jnp.where(place < w4 - 1, pltpu.roll(terms[2], tall * w4 - 1, 0), 0.0)
    ).astype(jnp.bfloat16)
    for part in range(count_c):
        sendt[part] = dot(pick_top[part * wide_t : (part + 1) * wide_t], partial).astype(
            jnp.bfloat16
        )
    top_copies = []
    for step in range(1, count_c):
        there = lax.rem(col + step, count_c)
        copy = remote(sendt.at[there], gott.at[col], sem_top, step - 1, {"col": there})
        copy.start()
        top_copies.append(copy)
    gott[pl.ds(col, 1)] = sendt[pl.ds(col, 1)]

    when_each(has_right, left_copies, "wait_recv")
    when_each(has_left, right_copies, "wait_recv")
    for frame, h, w, incoming in ((f1, h1 + 4, w1, in1), (f2, h2 + 4, w2, in2)):
        count, depth = incoming.shape[1:]
        value = dot(column_pick(h, count, EDGE - 2, True), incoming[0])
        frame[:, 0:EDGE] = value.astype(jnp.bfloat16).reshape(h, EDGE, depth)
        value = dot(column_pick(h, count, 0, True), incoming[1])
        frame[:, EDGE + w :] = value.astype(jnp.bfloat16).reshape(h, EDGE, depth)
    when_each(has_down, [up3], "wait_recv")
    when_each(has_up, [down3], "wait_recv")
    later()

    for copy in top_copies:
        copy.wait_recv()
    total = gott[0].astype(jnp.float32)
    for part in range(1, count_c):
        total = total + gott[part].astype(jnp.float32)
    top[...] = jnp.maximum(total + offsets[4:5], 0.0).astype(jnp.bfloat16)

    for copy in four_copies + bin_copies + three_copies + top_copies:
        copy.wait_send()
    when_each(has_up, up_copies + [up3], "wait_send")
    when_each(has_down, down_copies + [down3], "wait_send")
    when_each(has_left, left_copies, "wait_send")
    when_each(has_right, right_copies, "wait_send")


def column_matrix(col, own, first, width, own_from, first_from, width_from, factor, total):
    place = col * own + first + lax.broadcasted_iota(jnp.int32, (width, width_from), 0)
    source = (place.astype(jnp.float32) + 0.5) / factor - 0.5
    source = jnp.clip(source, 0.0, total // factor - 1.0)
    here = col * own_from + first_from + lax.broadcasted_iota(jnp.int32, (width, width_from), 1)
    weight = jnp.maximum(0.0, 1.0 - jnp.abs(source - here.astype(jnp.float32)))
    return jnp.where((place >= 0) & (place < total), weight, 0.0).astype(jnp.bfloat16)


def back(
    sizes, f1, f2, t3, top, offsets, fetches, out, lat1, lat2, lat3, smooth, join,
    p3, p2, p1, s3, s2, joint, wide, term3, term2, term1,
):
    count_r, count_c = sizes
    row, col = lax.axis_index("row"), lax.axis_index("col")
    at_top, at_bottom = row == 0, row == count_r - 1
    h1, w1, channels = out.shape
    h2, w2, h3, w3, h4, w4 = h1 // 2, w1 // 2, h1 // 4, w1 // 4, h1 // 8, w1 // 8
    n1, n2, n3 = w1 + 16, w2 + 16, p3.shape[1]
    n4 = top.shape[0] // (h4 + 4)
    pack3 = t3.shape[1] // (h3 + 4)

    def inside(first, width, own):
        place = col * own + first + lax.broadcasted_iota(jnp.int32, (1, width, 1), 1)
        return (place >= 0) & (place < own * count_c)

    def row_inside(t, h):
        if t < 0:
            return jnp.logical_not(at_top)
        if t >= h:
            return jnp.logical_not(at_bottom)
        return None

    def widen(read, matrix, h, border):
        width = matrix.shape[0]
        for r in range(h + 2 * border):
            wide[r, 0:width] = dot(matrix, read(r))

        @pl.when(at_top)
        def _():
            wide[border - 1, 0:width] = wide[border, 0:width]

        @pl.when(at_bottom)
        def _():
            wide[border + h, 0:width] = wide[border + h - 1, 0:width]

    def interpolate(t, factor, border, width):
        source = (t + 0.5) / factor - 0.5
        low = int(np.floor(source))
        weight = float(source - low)
        return (
            wide[border + low, 0:width] * (1.0 - weight)
            + wide[border + low + 1, 0:width] * weight
        )

    def store_row(target, index, value, t, h, lanes=slice(None)):
        keep = row_inside(t, h)
        if keep is not None:
            value = jnp.where(keep, value, 0.0)
        target[index, :, lanes] = value.astype(jnp.bfloat16)

    def taps(read, weight, stride, rows):
        size = rows * stride
        sums = []
        for dx in range(3):
            total = None
            for dy in range(3):
                term = dot(read(dy), weight(dy, dx))
                total = term if total is None else total + term
            sums.append(total)
        return sums[1] + pltpu.roll(sums[0], 1, 0) + pltpu.roll(sums[2], size - 1, 0)

    term = term3
    keep = inside(-4, n3, w3)
    widen(lambda r: top[r * n4 : (r + 1) * n4],
          column_matrix(col, w3, -4, n3, w4, -4, n4, 2, w3 * count_c), h4, 2)
    for t in range(-2, h3 + 2):
        value = jnp.where(keep[0], term[t + 2] + interpolate(t, 2, 2, n3), 0.0)
        store_row(p3, t + 2, value, t, h3)

    term = term2
    keep = inside(-8, n2, w2)
    widen(lambda r: p3[r], column_matrix(col, w2, -8, n2, w3, -4, n3, 2, w2 * count_c), h3, 2)
    for t in range(-2, h2 + 2):
        value = jnp.where(keep[0], term[t + 2] + interpolate(t, 2, 2, n2), 0.0)
        store_row(p2, t + 2, value, t, h2)

    keep = inside(-8, n1, w1)
    widen(lambda r: p2[r], column_matrix(col, w1, -8, n1, w2, -8, n2, 2, w1 * count_c), h2, 2)
    for t in range(-2, h1 + 2):
        value = jnp.where(keep[0], term1[t + 2] + interpolate(t, 2, 2, n1), 0.0)
        store_row(p1, t + 2, value, t, h1)

    fetches[3].wait()
    value = taps(lambda dy: p3[dy : dy + h3 + 2].reshape((h3 + 2) * n3, channels),
                 lambda dy, dx: smooth[2, dy, dx], n3, h3 + 2)
    s3[...] = jnp.maximum(value + offsets[10:11], 0.0).astype(jnp.bfloat16).reshape(s3.shape)
    value = taps(lambda dy: p2[dy : dy + h2 + 2].reshape((h2 + 2) * n2, channels),
                 lambda dy, dx: smooth[1, dy, dx], n2, h2 + 2)
    s2[...] = jnp.maximum(value + offsets[9:10], 0.0).astype(jnp.bfloat16).reshape(s2.shape)

    group = 6
    @pl.loop(0, (h1 + 2) // group)
    def _(block):
        value = taps(
            lambda dy: p1[pl.ds(block * group + dy, group)].reshape(group * n1, channels),
            lambda dy, dx: smooth[0, dy, dx], n1, group,
        )
        value = jnp.maximum(value + offsets[8:9], 0.0).reshape(group, n1, channels)
        value = jnp.where(keep, value, 0.0)
        joint[pl.ds(block * group, group), :, 0:channels] = value.astype(jnp.bfloat16)

    @pl.when(at_top)
    def _():
        joint[0, :, 0:channels] = jnp.zeros((n1, channels), jnp.bfloat16)

    @pl.when(at_bottom)
    def _():
        joint[h1 + 1, :, 0:channels] = jnp.zeros((n1, channels), jnp.bfloat16)

    total1 = w1 * count_c
    for number, (read, matrix, factor, h, border) in enumerate((
        (lambda r: s2[r], column_matrix(col, w1, -8, n1, w2, -8, n2, 2, total1), 2, h2, 1),
        (lambda r: s3[r], column_matrix(col, w1, -8, n1, w3, -4, n3, 4, total1), 4, h3, 1),
        (lambda r: top[r * n4 : (r + 1) * n4],
         column_matrix(col, w1, -8, n1, w4, -4, n4, 8, total1), 8, h4, 2),
    )):
        widen(read, matrix, h, border)
        lanes = slice((number + 1) * channels, (number + 2) * channels)
        for t in range(-1, h1 + 1):
            store_row(joint, t + 1, interpolate(t, factor, border, n1), t, h1, lanes)

    fetches[4].wait()
    rows = 4
    @pl.loop(0, h1 // rows)
    def _(block):
        value = taps(
            lambda dy: joint[pl.ds(block * rows + dy, rows)].reshape(rows * n1, joint.shape[2]),
            lambda dy, dx: join[dy, dx], n1, rows,
        )
        value = jnp.maximum(value + offsets[11:12], 0.0).reshape(rows, n1, channels)
        out[pl.ds(block * rows, rows)] = value[:, 8 : 8 + w1].astype(jnp.bfloat16)


def laterals(f1, f2, t3, offsets, fetches, lat1, lat2, lat3, term3, term2, term1):
    for copy in fetches[0:3]:
        copy.wait()
    share = t3.shape[2]
    term = None
    for part in range(t3.shape[0]):
        piece = dot(t3[part], lat3[part * share : (part + 1) * share])
        term = piece if term is None else term + piece
    rows, width, channels = term3.shape
    packed = t3.shape[1] // rows
    term3[:, 0:packed] = jnp.maximum(term + offsets[7:8], 0.0).reshape(rows, packed, channels)
    term3[:, packed:] = jnp.zeros((rows, width - packed, channels), jnp.float32)
    for frame, weight, line, target in ((f2, lat2, 6, term2), (f1, lat1, 5, term1)):
        for r in range(frame.shape[0]):
            term = jnp.maximum(dot(frame[r], weight[...]) + offsets[line : line + 1], 0.0)
            target[r] = term[8 : 8 + target.shape[1]]


def head(sizes, *refs):
    inputs, (lat1_h, lat2_h, lat3_h, smooth_h, join_h), out = refs[:13], refs[13:18], refs[18]
    f1, f2, t3, top = refs[19:23]
    scratch, weights, maps, terms, sems = (
        refs[23:51], refs[51:56], refs[56:63], refs[63:66], refs[66]
    )
    lat1, lat2, lat3, smooth, join = weights
    offsets = scratch[4]
    fetches = [
        pltpu.make_async_copy(source, target, sems.at[number])
        for number, (source, target) in enumerate((
            (lat3_h, lat3), (lat2_h, lat2), (lat1_h, lat1), (smooth_h, smooth), (join_h, join),
        ))
    ]

    def early():
        for copy in fetches:
            copy.start()

    def later():
        laterals(f1, f2, t3, offsets, fetches, lat1, lat2, lat3, *terms)

    front(sizes, *inputs, f1, f2, t3, top, *scratch, early, later)
    back(sizes, f1, f2, t3, top, offsets, fetches, out, *weights, *maps, *terms)


def local(
    sizes, level_one, level_two, level_three, level_four, bin_weight, neck_feature, neck_pooled,
    lateral_one, lateral_two, lateral_three, smooth_weight, join_weight, biases,
):
    count_r, count_c = sizes
    h1, w1, c1 = level_one.shape
    h2, w2, c2 = level_two.shape
    h3, wide3, c3 = level_three.shape
    h4, wide4, c4 = level_four.shape
    channels = bin_weight.shape[2]
    share = neck_pooled.shape[2]
    w3, w4 = wide3 // count_c, wide4 // count_c
    bf16, f32 = jnp.bfloat16, jnp.float32
    grid_rows = h4 * count_r
    member, scale = pool_counts(grid_rows, wide4)
    spread = spread_table(grid_rows, wide4, 3)
    pack3, pack4 = w3 + 8, w4 + 8
    pick_top = pick_table(h4 + 4, wide4, count_c, -4, pack4)
    pick_three = pick_table(h3, wide3, count_c, -4, pack3)
    vmem = pl.BlockSpec(memory_space=pltpu.VMEM)
    hbm = pl.BlockSpec(memory_space=pltpu.HBM)
    dma = pltpu.SemaphoreType.DMA
    steps_r, steps_c = max(count_r - 1, 1), max(count_c - 1, 1)
    column1, column2 = round_up(2 * (h1 + 4), 16), round_up(2 * (h2 + 4), 16)
    n1, n2, n3 = w1 + 16, w2 + 16, round_up(pack3, 16)
    return pl.pallas_call(
        functools.partial(head, sizes),
        out_shape=jax.ShapeDtypeStruct((h1, w1, channels), bf16),
        in_specs=[hbm] * 18,
        out_specs=vmem,
        scratch_shapes=[
            pltpu.VMEM((h1 + 4, w1 + 2 * EDGE, c1), bf16),
            pltpu.VMEM((h2 + 4, w2 + 2 * EDGE, c2), bf16),
            pltpu.VMEM((count_c, (h3 + 4) * pack3, c3), bf16),
            pltpu.VMEM(((h4 + 4) * pack4, channels), bf16),
            pltpu.VMEM(level_three.shape, bf16),
            pltpu.VMEM(bin_weight.shape, bf16),
            pltpu.VMEM(neck_feature.shape, bf16),
            pltpu.VMEM(neck_pooled.shape, bf16),
            pltpu.VMEM(biases.shape, f32),
            pltpu.VMEM(member.shape, bf16),
            pltpu.VMEM(scale.shape, f32),
            pltpu.VMEM(((h4 + 6) * wide4, CELLS), f32),
            pltpu.VMEM(pick_top.shape, bf16),
            pltpu.VMEM(pick_three.shape, bf16),
            pltpu.VMEM((grid_rows + 6, wide4, c4), bf16),
            pltpu.VMEM((count_c, h3 * pack3, c3), bf16),
            pltpu.VMEM((count_c, CELLS, share), bf16),
            pltpu.VMEM((count_c, CELLS, share), bf16),
            pltpu.VMEM((count_c, (h4 + 4) * pack4, channels), bf16),
            pltpu.VMEM((count_c, (h4 + 4) * pack4, channels), bf16),
            pltpu.VMEM((h4 + 6, wide4, share), bf16),
            pltpu.VMEM((2, column1, c1), bf16),
            pltpu.VMEM((2, column1, c1), bf16),
            pltpu.VMEM((2, column2, c2), bf16),
            pltpu.VMEM((2, column2, c2), bf16),
            dma((13,)),
            dma((2, steps_r)),
            dma((2, 6)),
            dma((2, 4)),
            dma((2, steps_c)),
            dma((2, steps_c)),
            dma((2, steps_c)),
            pltpu.VMEM(lateral_one.shape, bf16),
            pltpu.VMEM(lateral_two.shape, bf16),
            pltpu.VMEM(lateral_three.shape, bf16),
            pltpu.VMEM(smooth_weight.shape, bf16),
            pltpu.VMEM(join_weight.shape, bf16),
            pltpu.VMEM((h3 + 4, n3, channels), bf16),
            pltpu.VMEM((h2 + 4, n2, channels), bf16),
            pltpu.VMEM((h1 + 4, n1, channels), bf16),
            pltpu.VMEM((h3 + 2, n3, channels), bf16),
            pltpu.VMEM((h2 + 2, n2, channels), bf16),
            pltpu.VMEM((h1 + 2, n1, 4 * channels), bf16),
            pltpu.VMEM((h2 + 4, n1, channels), f32),
            pltpu.VMEM((h3 + 4, n3, channels), f32),
            pltpu.VMEM((h2 + 4, n2, channels), f32),
            pltpu.VMEM((h1 + 4, n1, channels), f32),
            dma((5,)),
        ],
        compiler_params=pltpu.CompilerParams(
            collective_id=0, has_side_effects=True, vmem_limit_bytes=60 * 1024 * 1024
        ),
        name="head",
    )(
        level_one, level_two, level_three, level_four, bin_weight, neck_feature, neck_pooled,
        biases, jnp.asarray(member, bf16), jnp.asarray(scale), jnp.asarray(spread),
        jnp.asarray(pick_top, bf16), jnp.asarray(pick_three, bf16),
        lateral_one, lateral_two, lateral_three, smooth_weight, join_weight,
    )


def solution(mesh):
    placed = (
        P(("grp", "row"), "col", None),
        P(("grp", "row"), "col", None),
        P(("grp", "row"), None, "col"),
        P(("grp", "row"), None, "col"),
        P(None, "col", None),
        P(None, None, "col", None),
        P(None, None, "col", None),
        P(),
        P(),
        P(),
        P(),
        P(),
        P(),
    )
    sizes = (mesh.shape["row"], mesh.shape["col"])
    return jax.shard_map(
        functools.partial(local, sizes), mesh=mesh, in_specs=placed,
        out_specs=P(("grp", "row"), "col", None), check_vma=False,
    )
```
